32 devices in a mesh: dp: 8 (over y, x, core), tensor: 4 (over z).
Axes of the slice: x: 2, y: 2, z: 4, core: 2. Of those that a mesh axis runs over, the one named last changes fastest.
Arguments:
- tokens: bfloat16 [16384, 1024], P(('dp', 'tensor')), may hold values from -6 to 6
- w_qkv: bfloat16 [3, 1024, 1024], P(None, 'dp', 'tensor'), may hold values from -0.1875 to 0.1875
- w_attn_out: bfloat16 [1024, 1024], P('dp', 'tensor'), may hold values from -1.5 to 1.5
- w_in: bfloat16 [1024, 4096], P('dp', 'tensor'), may hold values from -0.1875 to 0.1875
- w_out: bfloat16 [1024, 4096], P('dp', 'tensor'), may hold values from -0.09375 to 0.09375
- b_qv: bfloat16 [2, 1024], P(None, 'dp'), may hold values from -0.59765625 to 0.59765625
- b_proj: bfloat16 [2, 1024], P(None, 'dp'), may hold values from -3 to 3
- b_hidden: bfloat16 [4096], P('dp'), may hold values from -3 to 3
- ln_gain: bfloat16 [2, 1024], P(None, 'dp'), may hold values from 0.25 to 1.75
- ln_bias: bfloat16 [2, 1024], P(None, 'dp'), may hold values from -2 to 2
- doc_lengths: int32 [8, 4], P('dp'), may hold values from 1 to 1600, 2048 in all within a row
- cotangent: bfloat16 [16384, 1024], P(('dp', 'tensor')), may hold values from -6 to 6
Outputs:
- output: bfloat16 [16384, 1024], P(('dp', 'tensor'))
- grad_tokens: bfloat16 [16384, 1024], P(('dp', 'tensor'))
- grad_qkv: float32 [3, 1024, 1024], P(None, 'dp', 'tensor')
- grad_attn_out: float32 [1024, 1024], P('dp', 'tensor')
- grad_in: float32 [1024, 4096], P('dp', 'tensor')
- grad_out: float32 [1024, 4096], P('dp', 'tensor')
- grad_qv: float32 [2, 1024], P(None, 'dp')
- grad_proj: float32 [2, 1024], P(None, 'dp')
- grad_hidden: float32 [4096], P('dp')
- grad_gain: float32 [2, 1024], P(None, 'dp')
- grad_shift: float32 [2, 1024], P(None, 'dp')
The draws below stay inside these ranges and needn't reach their ends.
Inputs may be any that keep to these rules, and one draw needn't show every extreme that they name: `doc_lengths`: row s holds the lengths of the 4 documents packed into sequence s, in order; they sum to 2048, and the longest of each row is exactly 1600.
All inputs are finite; a program needn't handle non-finite values.
Results may differ from the reference program's by a relative error of at most 0.02.
Values may be sent and summed in bfloat16 or wider, within the bound.
A program may use at most 128 MiB of HBM per device.

```python
import math
import jax
import jax.numpy as jnp
import numpy as np
from jax import lax

D = 1024
H = 16
HD = 64
FF = 4096
LEN = 2048
DOCS = 4
MOST = 1600
SEQS = 8
TOKENS = 16384


def raised(values, rng, source, target, blocks, factor):
    owner, partner = [(jnp.arange(values.shape[axis_at]) // (values.shape[axis_at] // blocks)).reshape([-1 if axis == axis_at else 1 for axis in range(values.ndim)]) for axis_at in (source, target)]
    chosen = jax.random.permutation(rng, blocks)[partner]
    strong = (owner == chosen) | (owner == (partner + blocks // 2) % blocks)
    return jnp.where(strong, factor * values, values)


def block_levels(rng, shape, pieces, low, high):
    loudness = 1.0
    for axis_at, shards_of in pieces:
        heights = jax.random.uniform(jax.random.fold_in(jax.random.fold_in(rng, 6), axis_at), (shards_of,), jnp.float32, low / len(pieces), high / len(pieces))
        loudness = loudness * jnp.repeat(jnp.exp(heights), shape[axis_at] // shards_of).reshape((-1,) + (1,) * (len(shape) - 1 - axis_at))
    return loudness


def length_profile(amount, total, limit, slope):
    weights = [(1 << 20) // math.isqrt(standing ** slope) + 1 for standing in range(2, amount + 1)]
    rest, given = total - limit - (amount - 1), [1] * (amount - 1)
    while rest > 0:
        free = [i for i in range(amount - 1) if given[i] < limit]
        mass, remaining = sum([weights[i] for i in free]), rest
        for i in free:
            more = min(limit - given[i], max(1, remaining * weights[i] // mass), rest)
            given[i] = given[i] + more
            rest = rest - more
    return np.array([limit] + given)


def ragged(rng, number_of, total, reach, skew):
    if number_of == 2:
        one = jax.random.randint(rng, (), max(1, total - reach), min(reach, total - 1) + 1)
        return jnp.stack([one, total - one])
    sizes = jnp.asarray(length_profile(number_of, total, reach, skew), jnp.int32)
    couples = (number_of - 1) // 2
    source_of, sink = sizes[1:1 + 2 * couples:2], sizes[2:2 + 2 * couples:2]
    room = jnp.minimum(source_of - 1, reach - sink)
    passed = jax.random.randint(jax.random.fold_in(rng, 1), (couples,), 0, 1 << 20) % (room + 1)
    sizes = sizes.at[1:1 + 2 * couples:2].set(source_of - passed).at[2:2 + 2 * couples:2].set(sink + passed)
    return sizes[jax.random.permutation(jax.random.fold_in(rng, 2), number_of)]


def bell_draw(key, dims, scale, limit, pieces=(), held_as=jnp.bfloat16):
    values = jax.random.normal(key, dims, jnp.float32) * scale
    if len(pieces) > 0:
        values = block_levels(key, dims, pieces, -0.22, 0.18) * values
    return jnp.clip(values, min=-limit, max=limit).astype(held_as)


def noise_with(stream_key, dims, scale, most, cuts, heavy, held_as=jnp.bfloat16):
    values = scale * jax.random.normal(stream_key, dims, jnp.float32)
    if cuts:
        values = values * block_levels(stream_key, dims, cuts, -0.22, 0.18)
    return jnp.clip(raised(values, jax.random.fold_in(stream_key, 3), *heavy), -most, most).astype(held_as)


def setup_inputs(seed: int = 0) -> dict:
    key_of = jax.random.split(jax.random.key(seed), 13)
    tokens = noise_with(key_of[0], (TOKENS, D), 1.0, 6.0, ((0, 32),), (0, 1, 32, 2.75))
    w_qkv = bell_draw(key_of[1], (3, D, D), D ** -0.5, 0.1875, ((1, 8), (2, 4)))
    w_attn_out = bell_draw(key_of[2], (D, D), 16 ** -0.5, 1.5, ((0, 8), (1, 4)))
    w_in = bell_draw(key_of[3], (D, FF), D ** -0.5, 0.1875, ((0, 8), (1, 4)))
    w_out = bell_draw(key_of[4], (D, FF), FF ** -0.5, 0.09375, ((0, 8), (1, 4)))
    b_qv = bell_draw(key_of[5], (2, D), 0.1, 0.59765625, ((1, 8),))
    b_proj = bell_draw(key_of[6], (2, D), 0.5, 3.0, ((1, 8),))
    b_hidden = bell_draw(key_of[7], (FF,), 0.5, 3.0, ((0, 8),))
    ln_gain = jnp.clip(1.0 + 0.15 * jax.random.normal(key_of[8], (2, D), jnp.float32), 0.25, 1.75).astype(jnp.bfloat16)
    ln_bias = bell_draw(key_of[9], (2, D), 0.3, 2.0, ((1, 8),))
    doc_lengths = jax.vmap(lambda own: ragged(own, DOCS, LEN, MOST, 2))(jax.random.split(key_of[10], SEQS)).reshape((SEQS, DOCS)).astype(jnp.int32)
    cotangent = noise_with(key_of[11], (TOKENS, D), 1.0, 6.0, ((0, 32),), (0, 1, 32, 2.75))
    return dict(tokens=tokens, w_qkv=w_qkv, w_attn_out=w_attn_out, w_in=w_in, w_out=w_out, b_qv=b_qv, b_proj=b_proj, b_hidden=b_hidden, ln_gain=ln_gain, ln_bias=ln_bias, doc_lengths=doc_lengths, cotangent=cotangent)


@jax.custom_vjp
def low(v):
    return lax.optimization_barrier(v.astype(jnp.bfloat16)).astype(jnp.float32)

@jax.custom_vjp
def low_back(v):
    return v

def low_keep(v):
    return (low(v), None)

def low_pass(kept, grad):
    return (grad,)

def back_keep(v):
    return (v, None)

def back_low(kept, grad):
    return (low(grad),)
low.defvjp(low_keep, low_pass)
low_back.defvjp(back_keep, back_low)
epsilon = 1e-06

def layer_norm(rows, gain, shift):
    centred = rows - lax.optimization_barrier(jnp.mean(rows, -1, keepdims=True))
    spread = lax.optimization_barrier(jnp.mean(centred * centred, -1, keepdims=True))
    return centred * lax.rsqrt(spread + epsilon) * gain + shift

def gelu_exact(values):
    return jax.nn.gelu(values, approximate=False)

def segment_ids(lengths, length):
    ends = jnp.cumsum(lengths, axis=-1).astype(jnp.int32)
    places = jnp.arange(length, dtype=jnp.int32)
    return lax.optimization_barrier(jnp.sum((places[None, :, None] >= ends[:, None, :]).astype(jnp.int32), -1)).astype(jnp.int32)

def forward_one(inputs, segments, w_qkv, w_attn_out, w_in, w_out, b_qv, b_proj, b_hidden, ln_gain, ln_bias):
    highest = lax.Precision.HIGHEST
    length = inputs.shape[0]
    queries = low_back(low(jnp.dot(inputs, w_qkv[0], precision=highest) + b_qv[0]))
    keys = low_back(low(jnp.dot(inputs, w_qkv[1], precision=highest)))
    values = low_back(low(jnp.dot(inputs, w_qkv[2], precision=highest) + b_qv[1]))
    split = (length, H, HD)
    scores = jnp.einsum('qhd,khd->hqk', queries.reshape(split), keys.reshape(split), precision=highest) * HD ** (-0.5)
    scores = low_back(scores)
    allowed = segments[:, None] == segments[None, :]
    scores = jnp.where(allowed[None], scores, -jnp.inf)
    peaks = lax.optimization_barrier(jnp.max(scores, -1, keepdims=True))
    powered = jnp.exp(scores - peaks)
    weights = powered / lax.optimization_barrier(jnp.sum(powered, -1, keepdims=True))
    context = jnp.einsum('hqk,khd->qhd', low(weights), values.reshape(split), precision=highest).reshape(length, H * HD)
    context = low_back(low(context))
    attended = low_back(jnp.dot(context, w_attn_out.T, precision=highest) + b_proj[0])
    normed = layer_norm(inputs + attended, ln_gain[0], ln_bias[0])
    hidden = low_back(jnp.dot(low(normed), w_in, precision=highest) + b_hidden)
    activated = low(gelu_exact(hidden))
    mixed = low_back(jnp.dot(activated, w_out.T, precision=highest) + b_proj[1])
    return layer_norm(normed + mixed, ln_gain[1], ln_bias[1])

def reference(tokens, w_qkv, w_attn_out, w_in, w_out, b_qv, b_proj, b_hidden, ln_gain, ln_bias, doc_lengths, cotangent):
    params = tuple((array.astype(jnp.float32) for array in (w_qkv, w_attn_out, w_in, w_out, b_qv, b_proj, b_hidden, ln_gain, ln_bias)))
    inputs = tokens.astype(jnp.float32).reshape(SEQS, LEN, D)
    incoming = cotangent.astype(jnp.float32).reshape(SEQS, LEN, D)
    segments = segment_ids(doc_lengths, LEN)

    def per_sequence(totals, packed):
        seq_rows, seg_row, grad_rows = packed

        def forward_rows(rows_in, *weights):
            return forward_one(rows_in, seg_row, *weights)
        result, pullback = jax.vjp(forward_rows, seq_rows, *params)
        grads = pullback(grad_rows)
        totals = tuple((total + grad for total, grad in zip(totals, grads[1:])))
        return (totals, (result, grads[0]))
    start = tuple((jnp.zeros_like(array) for array in params))
    totals, (outputs, grad_inputs) = lax.scan(per_sequence, start, (inputs, segments, incoming))
    return (outputs.reshape(TOKENS, D).astype(jnp.bfloat16), grad_inputs.reshape(TOKENS, D).astype(jnp.bfloat16), totals[0], totals[1], totals[2], totals[3], totals[4], totals[5], totals[6], totals[7], totals[8])
```

```python
import functools

import jax
import jax.numpy as jnp
from jax import lax
from jax.experimental import pallas as pl
from jax.experimental.pallas import tpu as pltpu
from jax.sharding import PartitionSpec as P

HD = 64
LEN = 2048


epsilon = 1e-06


def layer_norm(rows, gain, shift):
    centred = rows - jnp.mean(rows, -1, keepdims=True)
    spread = jnp.mean(centred * centred, -1, keepdims=True)
    return centred * lax.rsqrt(spread + epsilon) * gain + shift


def gelu_exact(values):
    return jax.nn.gelu(values, approximate=False)


def segment_ids(lengths, length):
    ends = jnp.cumsum(lengths, axis=-1)
    places = jnp.arange(length, dtype=jnp.int32)
    return jnp.sum((places[None, :, None] >= ends[:, None, :]).astype(jnp.int32), -1)


def matmul(left, right):
    return jnp.dot(left, right, preferred_element_type=jnp.float32)


def matmul_nt(left, right):
    return lax.dot_general(
        left, right, (((1,), (1,)), ((), ())), preferred_element_type=jnp.float32
    )


def matmul_tn(left, right):
    return lax.dot_general(
        left, right, (((0,), (0,)), ((), ())), preferred_element_type=jnp.float32
    )


def forward_kernel(heads, head_dim, block, ranges, q_t, k, v_t, seg_q, seg_k, ctx_t, lse):
    index = pl.program_id(0)
    low, high = ranges[0, index], ranges[1, index]
    local = heads * head_dim
    query = q_t[...]
    rows = lax.broadcasted_iota(jnp.int32, (local, block), 0) // head_dim
    masked = [jnp.where(rows == h, query, jnp.zeros_like(query)) for h in range(heads)]
    seg_row = seg_q[0:1, :]

    def step(j, carry):
        at = pl.ds(pl.multiple_of(j * block, block), block)
        keys = k[at, :]
        same = seg_k[at, :] == seg_row
        new = []
        for h in range(heads):
            peak, total, acc = carry[h]
            scores = jnp.dot(keys, masked[h], preferred_element_type=jnp.float32)
            scores = jnp.where(same, scores, -1e30)
            top = jnp.maximum(peak, jnp.max(scores, 0, keepdims=True))
            powered = jnp.exp(scores - top)
            shrink = jnp.exp(peak - top)
            total = total * shrink + jnp.sum(powered, 0, keepdims=True)
            part = jnp.dot(
                v_t[h * head_dim : (h + 1) * head_dim, at],
                powered.astype(jnp.bfloat16),
                preferred_element_type=jnp.float32,
            )
            new.append((top, total, acc * shrink + part))
        return tuple(new)

    first = tuple(
        (
            jnp.full((1, block), -1e30, jnp.float32),
            jnp.zeros((1, block), jnp.float32),
            jnp.zeros((head_dim, block), jnp.float32),
        )
        for _ in range(heads)
    )
    done = lax.fori_loop(low, high, step, first)
    for h in range(heads):
        peak, total, acc = done[h]
        ctx_t[h * head_dim : (h + 1) * head_dim, :] = acc / total
        lse[h : h + 1, :] = peak + jnp.log(total)


def backward_kernel(
    heads, head_dim, block, ranges, q_t, q, k, k_t, v, g_t, g, ctx_t, lse, seg_q, seg_k,
    dq_t, dk, dv, dk_sum, dv_sum,
):
    index = pl.program_id(0)
    low, high = ranges[0, index], ranges[1, index]
    local = heads * head_dim

    @pl.when(index == 0)
    def _():
        dk_sum[...] = jnp.zeros_like(dk_sum)
        dv_sum[...] = jnp.zeros_like(dv_sum)

    rows = lax.broadcasted_iota(jnp.int32, (local, block), 0) // head_dim
    lanes = lax.broadcasted_iota(jnp.int32, (block, local), 1) // head_dim
    query_t, query, grad_t, grad = q_t[...], q[...], g_t[...], g[...]
    zero_t, zero = jnp.zeros_like(query_t), jnp.zeros_like(query)
    products = grad_t.astype(jnp.float32) * ctx_t[...]
    inner = [
        jnp.sum(products[h * head_dim : (h + 1) * head_dim, :], 0, keepdims=True)
        for h in range(heads)
    ]
    qs_t = [jnp.where(rows == h, query_t, zero_t) for h in range(heads)]
    gs_t = [jnp.where(rows == h, grad_t, zero_t) for h in range(heads)]
    qs = [jnp.where(lanes == h, query, zero) for h in range(heads)]
    gs = [jnp.where(lanes == h, grad, zero) for h in range(heads)]
    seg_row = seg_q[0:1, :]

    def step(j, carry):
        at = pl.ds(pl.multiple_of(j * block, block), block)
        keys, vals = k[at, :], v[at, :]
        same = seg_k[at, :] == seg_row
        new = []
        d_keys = jnp.zeros((block, local), jnp.float32)
        d_vals = jnp.zeros((block, local), jnp.float32)
        for h in range(heads):
            scores = jnp.dot(keys, qs_t[h], preferred_element_type=jnp.float32)
            weights = jnp.exp(jnp.where(same, scores - lse[h : h + 1, :], -1e30))
            d_weights = jnp.dot(vals, gs_t[h], preferred_element_type=jnp.float32)
            d_scores = (weights * (d_weights - inner[h])).astype(jnp.bfloat16)
            d_vals += jnp.dot(
                weights.astype(jnp.bfloat16), gs[h], preferred_element_type=jnp.float32
            )
            d_keys += jnp.dot(d_scores, qs[h], preferred_element_type=jnp.float32)
            new.append(
                carry[h]
                + jnp.dot(
                    k_t[h * head_dim : (h + 1) * head_dim, at],
                    d_scores,
                    preferred_element_type=jnp.float32,
                )
            )
        dk_sum[at, :] += d_keys
        dv_sum[at, :] += d_vals
        return tuple(new)

    first = tuple(jnp.zeros((head_dim, block), jnp.float32) for _ in range(heads))
    done = lax.fori_loop(low, high, step, first)
    for h in range(heads):
        dq_t[h * head_dim : (h + 1) * head_dim, :] = (done[h] * head_dim**-0.5).astype(
            jnp.bfloat16
        )

    @pl.when(index == pl.num_programs(0) - 1)
    def _():
        dk[...] = dk_sum[...].astype(jnp.bfloat16)
        dv[...] = dv_sum[...].astype(jnp.bfloat16)


def whole(shape):
    return pl.BlockSpec(shape, lambda i: (0, 0))


def attend_forward(ranges, q_t, k, v_t, seg_q, seg_k, head_dim, block):
    local, length = q_t.shape
    heads = local // head_dim
    cols = pl.BlockSpec((local, block), lambda i: (0, i))
    few = pl.BlockSpec((8, block), lambda i: (0, i))
    return pl.pallas_call(
        functools.partial(forward_kernel, heads, head_dim, block),
        grid=(length // block,),
        in_specs=[
            pl.BlockSpec(memory_space=pltpu.SMEM),
            cols,
            whole((length, local)),
            whole((local, length)),
            few,
            whole((length, 1)),
        ],
        out_specs=[cols, few],
        out_shape=[
            jax.ShapeDtypeStruct((local, length), jnp.float32),
            jax.ShapeDtypeStruct((8, length), jnp.float32),
        ],
        compiler_params=pltpu.CompilerParams(vmem_limit_bytes=48 * 2**20),
        cost_estimate=pl.CostEstimate(
            flops=16 * length * length * local,
            bytes_accessed=8 * length * local,
            transcendentals=heads * length * length,
        ),
    )(ranges, q_t, k, v_t, seg_q, seg_k)


def attend_backward(ranges, q_t, q, k, k_t, v, g_t, g, ctx_t, lse, seg_q, seg_k, head_dim, block):
    local, length = q_t.shape
    heads = local // head_dim
    cols = pl.BlockSpec((local, block), lambda i: (0, i))
    rows = pl.BlockSpec((block, local), lambda i: (i, 0))
    few = pl.BlockSpec((8, block), lambda i: (0, i))
    tall, wide = whole((length, local)), whole((local, length))
    return pl.pallas_call(
        functools.partial(backward_kernel, heads, head_dim, block),
        grid=(length // block,),
        in_specs=[
            pl.BlockSpec(memory_space=pltpu.SMEM),
            cols, rows, tall, wide, tall, cols, rows, cols, few, few,
            whole((length, 1)),
        ],
        out_specs=[cols, tall, tall],
        out_shape=[
            jax.ShapeDtypeStruct((local, length), jnp.bfloat16),
            jax.ShapeDtypeStruct((length, local), jnp.bfloat16),
            jax.ShapeDtypeStruct((length, local), jnp.bfloat16),
        ],
        scratch_shapes=[
            pltpu.VMEM((length, local), jnp.float32),
            pltpu.VMEM((length, local), jnp.float32),
        ],
        compiler_params=pltpu.CompilerParams(vmem_limit_bytes=48 * 2**20),
        cost_estimate=pl.CostEstimate(
            flops=40 * length * length * local,
            bytes_accessed=16 * length * local,
            transcendentals=heads * length * length,
        ),
    )(ranges, q_t, q, k, k_t, v, g_t, g, ctx_t, lse, seg_q, seg_k)


def column_sum(array):
    return jnp.sum(array.astype(jnp.float32), 0)


def dot(left, right, left_at, right_at):
    return lax.dot_general(
        left, right, (((left_at,), (right_at,)), ((), ())), preferred_element_type=jnp.float32
    )


def on_device(
    tokens,
    w_qkv,
    w_attn_out,
    w_in,
    w_out,
    b_qv,
    b_proj,
    b_hidden,
    ln_gain,
    ln_bias,
    doc_lengths,
    cotangent,
):
    head_dim = HD
    low = jnp.bfloat16
    rows_here, width = tokens.shape
    members = lax.axis_size("tensor")
    groups = lax.axis_size("dp")
    position = lax.axis_index("tensor")
    place = lax.axis_index("dp")
    part, local = w_qkv.shape[1:]
    hidden_all = w_in.shape[1] * members
    block = 256

    vectors = jnp.concatenate(
        [a.reshape(-1) for a in (b_qv, b_proj, ln_gain, ln_bias, b_hidden)]
    )
    inputs = lax.all_gather(tokens, "tensor", axis=0, tiled=True)
    lead = -(-vectors.size // local)
    lead += -lead % 16
    packed = jnp.concatenate(
        [
            w_qkv.reshape(3 * part, local),
            jnp.pad(vectors, (0, lead * local - vectors.size)).reshape(lead, local),
        ]
    )
    packed = lax.all_gather(packed, "dp", axis=0, tiled=False)
    qkv_all = (
        packed[:, : 3 * part]
        .reshape(groups, 3, part, local)
        .transpose(1, 0, 2, 3)
        .reshape(3, width, local)
    )
    vectors = packed[:, 3 * part :].reshape(groups, lead * local)

    def pairs(index):
        pieces = vectors[:, 2 * part * index : 2 * part * (index + 1)]
        pieces = pieces.reshape(groups, 2, part).transpose(1, 0, 2)
        return pieces.reshape(2, width).astype(jnp.float32)

    qv_bias, proj_bias, gains, shifts = (pairs(index) for index in range(4))
    hidden_bias = vectors[:, 8 * part : 8 * part + b_hidden.size].reshape(-1).astype(jnp.float32)
    query_bias = lax.dynamic_slice_in_dim(qv_bias[0], position * local, local)
    value_bias = lax.dynamic_slice_in_dim(qv_bias[1], position * local, local)

    def everywhere(w):
        w = lax.all_gather(w, "tensor", axis=1, tiled=True)
        return lax.all_gather(w, "dp", axis=0, tiled=True)

    attn_out_all, in_all, out_all = everywhere(w_attn_out), everywhere(w_in), everywhere(w_out)

    segments = segment_ids(doc_lengths, LEN)[0]
    seg_k = segments[:, None]
    seg_q = jnp.broadcast_to(segments[None, :], (8, LEN))
    ends = jnp.cumsum(doc_lengths[0])
    starts = jnp.arange(LEN // block, dtype=jnp.int32)[:, None] * block
    lows = jnp.max(jnp.where(ends[None, :] <= starts, ends[None, :], 0), -1)
    highs = jnp.min(jnp.where(ends[None, :] >= starts + block, ends[None, :], LEN), -1)
    ranges = jnp.stack([lows // block, (highs + block - 1) // block]).astype(jnp.int32)

    queries = (matmul(inputs, qkv_all[0]) + query_bias).astype(low) * jnp.asarray(
        head_dim**-0.5, low
    )
    keys = matmul(inputs, qkv_all[1]).astype(low)
    values = (matmul(inputs, qkv_all[2]) + value_bias).astype(low)
    queries_t, keys_t, values_t = queries.T, keys.T, values.T
    context_t, log_sums = attend_forward(
        ranges, queries_t, keys, values_t, seg_q, seg_k, head_dim, block
    )
    context = lax.all_to_all(
        context_t.T.astype(low).reshape(members, rows_here, local),
        "tensor", split_axis=0, concat_axis=0, tiled=False,
    )
    context = context.transpose(1, 0, 2).reshape(rows_here, width)
    attended = matmul_nt(context, attn_out_all) + proj_bias[0]
    normed_one, norm_one_pull = jax.vjp(
        layer_norm, tokens.astype(jnp.float32) + attended, gains[0], shifts[0]
    )
    normed = normed_one.astype(low)
    hidden_pre = matmul(normed, in_all) + hidden_bias
    activated, gelu_pull = jax.vjp(gelu_exact, hidden_pre)
    activated = activated.astype(low)
    mixed = matmul_nt(activated, out_all) + proj_bias[1]
    output, norm_two_pull = jax.vjp(layer_norm, normed_one + mixed, gains[1], shifts[1])
    grad_two, gain_two, shift_two = norm_two_pull(cotangent.astype(jnp.float32))
    grad_mixed = grad_two.astype(low)
    grad_pre = gelu_pull(matmul(grad_mixed, out_all))[0].astype(low)
    grad_normed = matmul_nt(grad_pre, in_all) + grad_two
    grad_one, gain_one, shift_one = norm_one_pull(grad_normed)
    grad_attended = grad_one.astype(low)
    grad_context = matmul(grad_attended, attn_out_all).astype(low)
    grad_context = lax.all_to_all(
        grad_context.reshape(rows_here, members, local).transpose(1, 0, 2),
        "tensor", split_axis=0, concat_axis=0, tiled=False,
    ).reshape(rows_here * members, local)

    def owned(grad):
        grad = lax.psum_scatter(grad.astype(low), "dp", scatter_dimension=0, tiled=True)
        grad = lax.psum_scatter(grad, "tensor", scatter_dimension=1, tiled=True)
        return grad.astype(jnp.float32)

    grad_in = owned(matmul_tn(normed, grad_pre))
    grad_out = owned(matmul_tn(grad_mixed, activated))
    grad_attn_out = owned(matmul_tn(grad_attended, context))

    grad_queries_t, grad_keys, grad_values = attend_backward(
        ranges, queries_t, queries, keys, keys_t, values, grad_context.T, grad_context,
        context_t, log_sums, seg_q, seg_k, head_dim, block,
    )
    total = dot(grad_queries_t, qkv_all[0], 0, 1)
    total = total + matmul_nt(grad_keys, qkv_all[1])
    total = total + matmul_nt(grad_values, qkv_all[2])
    grad_tokens = (
        lax.psum_scatter(
            total.astype(low), "tensor", scatter_dimension=0, tiled=True
        ).astype(jnp.float32)
        + grad_one
    ).astype(low)
    grad_qkv = jnp.stack(
        [
            dot(inputs, grad_queries_t, 0, 1),
            matmul_tn(inputs, grad_keys),
            matmul_tn(inputs, grad_values),
        ]
    ).astype(low)
    grad_qkv = lax.psum_scatter(grad_qkv, "dp", scatter_dimension=1, tiled=True)
    grad_qkv = grad_qkv.astype(jnp.float32)

    def placed(piece):
        return lax.dynamic_update_slice_in_dim(
            jnp.zeros((width,), jnp.float32), piece, position * local, 0
        )

    sums = jnp.concatenate(
        [
            jnp.stack(
                [
                    placed(jnp.sum(grad_queries_t.astype(jnp.float32), 1)),
                    placed(column_sum(grad_values)),
                    column_sum(grad_attended),
                    column_sum(grad_mixed),
                    gain_one,
                    gain_two,
                    shift_one,
                    shift_two,
                ]
            ),
            column_sum(grad_pre).reshape(-1, width),
        ]
    )
    sums = lax.psum(sums, ("dp", "tensor"))
    pieces = lax.dynamic_slice_in_dim(sums[:8], place * part, part, 1)
    grad_hidden = lax.dynamic_slice_in_dim(
        sums[8:].reshape(-1), place * b_hidden.size, b_hidden.size, 0
    )
    return (
        output.astype(low),
        grad_tokens,
        grad_qkv,
        grad_attn_out,
        grad_in,
        grad_out,
        pieces[0:2],
        pieces[2:4],
        grad_hidden,
        pieces[4:6],
        pieces[6:8],
    )


def solution(mesh):
    in_specs = (
        P(("dp", "tensor"), None),
        P(None, "dp", "tensor"),
        P("dp", "tensor"),
        P("dp", "tensor"),
        P("dp", "tensor"),
        P(None, "dp"),
        P(None, "dp"),
        P("dp"),
        P(None, "dp"),
        P(None, "dp"),
        P("dp", None),
        P(("dp", "tensor"), None),
    )
    out_specs = (
        P(("dp", "tensor"), None),
        P(("dp", "tensor"), None),
        P(None, "dp", "tensor"),
        P("dp", "tensor"),
        P("dp", "tensor"),
        P("dp", "tensor"),
        P(None, "dp"),
        P(None, "dp"),
        P("dp"),
        P(None, "dp"),
        P(None, "dp"),
    )
    return jax.shard_map(
        on_device, mesh=mesh, in_specs=in_specs, out_specs=out_specs, check_vma=False
    )
```

```python
import functools

import jax
import jax.numpy as jnp
from jax import lax
from jax.experimental import pallas as pl
from jax.experimental.pallas import tpu as pltpu
from jax.sharding import PartitionSpec as P

HD = 64
LEN = 2048


epsilon = 1e-06


def layer_norm(rows, gain, shift):
    centred = rows - jnp.mean(rows, -1, keepdims=True)
    spread = jnp.mean(centred * centred, -1, keepdims=True)
    return centred * lax.rsqrt(spread + epsilon) * gain + shift


def gelu_exact(values):
    return jax.nn.gelu(values, approximate=False)


def segment_ids(lengths, length):
    ends = jnp.cumsum(lengths, axis=-1)
    places = jnp.arange(length, dtype=jnp.int32)
    return jnp.sum((places[None, :, None] >= ends[:, None, :]).astype(jnp.int32), -1)


def matmul(left, right):
    return jnp.dot(left, right, preferred_element_type=jnp.float32)


def matmul_nt(left, right):
    return lax.dot_general(
        left, right, (((1,), (1,)), ((), ())), preferred_element_type=jnp.float32
    )


def matmul_tn(left, right):
    return lax.dot_general(
        left, right, (((0,), (0,)), ((), ())), preferred_element_type=jnp.float32
    )


def forward_kernel(heads, head_dim, block, ranges, q_t, k, v_t, seg_q, seg_k, ctx_t, lse):
    index = pl.program_id(0)
    low, high = ranges[0, index], ranges[1, index]
    local = heads * head_dim
    query = q_t[...]
    rows = lax.broadcasted_iota(jnp.int32, (local, block), 0) // head_dim
    wide = jnp.concatenate(
        [jnp.where(rows == h, query, jnp.zeros_like(query)) for h in range(heads)], 1
    )
    seg_row = jnp.concatenate([seg_q[0:1, :]] * heads, 1)

    def step(j, carry):
        peak, total, accs = carry
        at = pl.ds(pl.multiple_of(j * block, block), block)
        scores = jnp.dot(k[at, :], wide, preferred_element_type=jnp.float32)
        scores = jnp.where(seg_k[at, :] == seg_row, scores, -1e30)
        top = jnp.maximum(peak, jnp.max(scores, 0, keepdims=True))
        powered = jnp.exp(scores - top)
        shrink = jnp.exp(peak - top)
        total = total * shrink + jnp.sum(powered, 0, keepdims=True)
        powered = powered.astype(jnp.bfloat16)
        new = []
        for h in range(heads):
            cols = slice(h * block, (h + 1) * block)
            part = jnp.dot(
                v_t[h * head_dim : (h + 1) * head_dim, at],
                powered[:, cols],
                preferred_element_type=jnp.float32,
            )
            new.append(accs[h] * shrink[:, cols] + part)
        return top, total, tuple(new)

    first = (
        jnp.full((1, heads * block), -1e30, jnp.float32),
        jnp.zeros((1, heads * block), jnp.float32),
        tuple(jnp.zeros((head_dim, block), jnp.float32) for _ in range(heads)),
    )
    peak, total, accs = lax.fori_loop(low, high, step, first)
    log_sum = peak + jnp.log(total)
    for h in range(heads):
        cols = slice(h * block, (h + 1) * block)
        ctx_t[h * head_dim : (h + 1) * head_dim, :] = accs[h] / total[:, cols]
        lse[h : h + 1, :] = log_sum[:, cols]


def backward_kernel(
    heads, head_dim, block, ranges, q_t, q, k, k_t, v, g_t, g, ctx_t, lse, seg_q, seg_k,
    dq_t, dk, dv, dk_sum, dv_sum,
):
    index = pl.program_id(0)
    low, high = ranges[0, index], ranges[1, index]
    local = heads * head_dim

    @pl.when(index == 0)
    def _():
        dk_sum[...] = jnp.zeros_like(dk_sum)
        dv_sum[...] = jnp.zeros_like(dv_sum)

    rows = lax.broadcasted_iota(jnp.int32, (local, block), 0) // head_dim
    lanes = lax.broadcasted_iota(jnp.int32, (block, local), 1) // head_dim
    query_t, query, grad_t, grad = q_t[...], q[...], g_t[...], g[...]
    zero_t, zero = jnp.zeros_like(query_t), jnp.zeros_like(query)
    products = grad_t.astype(jnp.float32) * ctx_t[...]
    inner = jnp.concatenate(
        [
            jnp.sum(products[h * head_dim : (h + 1) * head_dim, :], 0, keepdims=True)
            for h in range(heads)
        ],
        1,
    )
    qs_t = jnp.concatenate([jnp.where(rows == h, query_t, zero_t) for h in range(heads)], 1)
    gs_t = jnp.concatenate([jnp.where(rows == h, grad_t, zero_t) for h in range(heads)], 1)
    qs = jnp.concatenate([jnp.where(lanes == h, query, zero) for h in range(heads)], 0)
    gs = jnp.concatenate([jnp.where(lanes == h, grad, zero) for h in range(heads)], 0)
    logs = jnp.concatenate([lse[h : h + 1, :] for h in range(heads)], 1)
    seg_row = jnp.concatenate([seg_q[0:1, :]] * heads, 1)

    def step(j, carry):
        at = pl.ds(pl.multiple_of(j * block, block), block)
        scores = jnp.dot(k[at, :], qs_t, preferred_element_type=jnp.float32)
        weights = jnp.exp(jnp.where(seg_k[at, :] == seg_row, scores - logs, -1e30))
        d_weights = jnp.dot(v[at, :], gs_t, preferred_element_type=jnp.float32)
        d_scores = (weights * (d_weights - inner)).astype(jnp.bfloat16)
        dv_sum[at, :] += jnp.dot(
            weights.astype(jnp.bfloat16), gs, preferred_element_type=jnp.float32
        )
        dk_sum[at, :] += jnp.dot(d_scores, qs, preferred_element_type=jnp.float32)
        return tuple(
            carry[h]
            + jnp.dot(
                k_t[h * head_dim : (h + 1) * head_dim, at],
                d_scores[:, h * block : (h + 1) * block],
                preferred_element_type=jnp.float32,
            )
            for h in range(heads)
        )

    first = tuple(jnp.zeros((head_dim, block), jnp.float32) for _ in range(heads))
    done = lax.fori_loop(low, high, step, first)
    for h in range(heads):
        dq_t[h * head_dim : (h + 1) * head_dim, :] = (done[h] * head_dim**-0.5).astype(
            jnp.bfloat16
        )

    @pl.when(index == pl.num_programs(0) - 1)
    def _():
        dk[...] = dk_sum[...].astype(jnp.bfloat16)
        dv[...] = dv_sum[...].astype(jnp.bfloat16)


def whole(shape):
    return pl.BlockSpec(shape, lambda i: (0, 0))


def attend_forward(ranges, q_t, k, v_t, seg_q, seg_k, head_dim, block):
    local, length = q_t.shape
    heads = local // head_dim
    cols = pl.BlockSpec((local, block), lambda i: (0, i))
    few = pl.BlockSpec((8, block), lambda i: (0, i))
    return pl.pallas_call(
        functools.partial(forward_kernel, heads, head_dim, block),
        grid=(length // block,),
        in_specs=[
            pl.BlockSpec(memory_space=pltpu.SMEM),
            cols,
            whole((length, local)),
            whole((local, length)),
            few,
            whole((length, 1)),
        ],
        out_specs=[cols, few],
        out_shape=[
            jax.ShapeDtypeStruct((local, length), jnp.float32),
            jax.ShapeDtypeStruct((8, length), jnp.float32),
        ],
        compiler_params=pltpu.CompilerParams(vmem_limit_bytes=48 * 2**20),
        cost_estimate=pl.CostEstimate(
            flops=16 * length * length * local,
            bytes_accessed=8 * length * local,
            transcendentals=heads * length * length,
        ),
    )(ranges, q_t, k, v_t, seg_q, seg_k)


def attend_backward(ranges, q_t, q, k, k_t, v, g_t, g, ctx_t, lse, seg_q, seg_k, head_dim, block):
    local, length = q_t.shape
    heads = local // head_dim
    cols = pl.BlockSpec((local, block), lambda i: (0, i))
    rows = pl.BlockSpec((block, local), lambda i: (i, 0))
    few = pl.BlockSpec((8, block), lambda i: (0, i))
    tall, wide = whole((length, local)), whole((local, length))
    return pl.pallas_call(
        functools.partial(backward_kernel, heads, head_dim, block),
        grid=(length // block,),
        in_specs=[
            pl.BlockSpec(memory_space=pltpu.SMEM),
            cols, rows, tall, wide, tall, cols, rows, cols, few, few,
            whole((length, 1)),
        ],
        out_specs=[cols, tall, tall],
        out_shape=[
            jax.ShapeDtypeStruct((local, length), jnp.bfloat16),
            jax.ShapeDtypeStruct((length, local), jnp.bfloat16),
            jax.ShapeDtypeStruct((length, local), jnp.bfloat16),
        ],
        scratch_shapes=[
            pltpu.VMEM((length, local), jnp.float32),
            pltpu.VMEM((length, local), jnp.float32),
        ],
        compiler_params=pltpu.CompilerParams(vmem_limit_bytes=48 * 2**20),
        cost_estimate=pl.CostEstimate(
            flops=40 * length * length * local,
            bytes_accessed=16 * length * local,
            transcendentals=heads * length * length,
        ),
    )(ranges, q_t, q, k, k_t, v, g_t, g, ctx_t, lse, seg_q, seg_k)


def column_sum(array):
    return jnp.sum(array.astype(jnp.float32), 0)


def dot(left, right, left_at, right_at):
    return lax.dot_general(
        left, right, (((left_at,), (right_at,)), ((), ())), preferred_element_type=jnp.float32
    )


def on_device(
    tokens,
    w_qkv,
    w_attn_out,
    w_in,
    w_out,
    b_qv,
    b_proj,
    b_hidden,
    ln_gain,
    ln_bias,
    doc_lengths,
    cotangent,
):
    head_dim = HD
    low = jnp.bfloat16
    rows_here, width = tokens.shape
    members = lax.axis_size("tensor")
    groups = lax.axis_size("dp")
    position = lax.axis_index("tensor")
    part, local = w_qkv.shape[1:]
    block = 256

    vectors = jnp.concatenate(
        [a.reshape(-1) for a in (b_qv, b_proj, ln_gain, ln_bias, b_hidden)]
    )
    inputs = lax.all_gather(tokens, "tensor", axis=0, tiled=True)
    lead = -(-vectors.size // local)
    lead += -lead % 16
    packed = jnp.concatenate(
        [
            w_qkv.reshape(3 * part, local),
            jnp.pad(vectors, (0, lead * local - vectors.size)).reshape(lead, local),
        ]
    )
    packed = lax.all_gather(packed, "dp", axis=0, tiled=False)
    shared = jnp.concatenate([w_attn_out.reshape(-1, w_in.shape[1]), w_in, w_out])
    shared = lax.all_to_all(
        jnp.broadcast_to(shared, (members, *shared.shape)),
        "tensor", split_axis=0, concat_axis=0, tiled=False,
    )
    inputs, packed, shared = lax.optimization_barrier((inputs, packed, shared))
    qkv_all = (
        packed[:, : 3 * part]
        .reshape(groups, 3, part, local)
        .transpose(1, 0, 2, 3)
        .reshape(3, width, local)
    )
    vectors = packed[:, 3 * part :].reshape(groups, lead * local)

    def pairs(index):
        pieces = vectors[:, 2 * part * index : 2 * part * (index + 1)]
        pieces = pieces.reshape(groups, 2, part).transpose(1, 0, 2)
        return pieces.reshape(2, width).astype(jnp.float32)

    qv_bias, proj_bias, gains, shifts = (pairs(index) for index in range(4))
    hidden_bias = vectors[:, 8 * part : 8 * part + b_hidden.size].reshape(-1).astype(jnp.float32)
    query_bias = lax.dynamic_slice_in_dim(qv_bias[0], position * local, local)
    value_bias = lax.dynamic_slice_in_dim(qv_bias[1], position * local, local)

    top = shared.shape[1] - 2 * part

    def everywhere(w):
        w = w.reshape(members, part, -1).transpose(1, 0, 2).reshape(part, -1)
        return lax.all_gather(w, "dp", axis=0, tiled=True)

    attn_out_all = everywhere(shared[:, :top])
    in_all = everywhere(shared[:, top : top + part])
    out_all = everywhere(shared[:, top + part :])

    segments = segment_ids(doc_lengths, LEN)[0]
    seg_k = segments[:, None]
    seg_q = jnp.broadcast_to(segments[None, :], (8, LEN))
    ends = jnp.cumsum(doc_lengths[0])
    starts = jnp.arange(LEN // block, dtype=jnp.int32)[:, None] * block
    lows = jnp.max(jnp.where(ends[None, :] <= starts, ends[None, :], 0), -1)
    highs = jnp.min(jnp.where(ends[None, :] >= starts + block, ends[None, :], LEN), -1)
    ranges = jnp.stack([lows // block, (highs + block - 1) // block]).astype(jnp.int32)

    queries = (matmul(inputs, qkv_all[0]) + query_bias).astype(low) * jnp.asarray(
        head_dim**-0.5, low
    )
    keys = matmul(inputs, qkv_all[1]).astype(low)
    values = (matmul(inputs, qkv_all[2]) + value_bias).astype(low)
    queries_t, keys_t, values_t = queries.T, keys.T, values.T
    context_t, log_sums = attend_forward(
        ranges, queries_t, keys, values_t, seg_q, seg_k, head_dim, block
    )
    context = lax.all_to_all(
        context_t.T.astype(low).reshape(members, rows_here, local),
        "tensor", split_axis=0, concat_axis=0, tiled=False,
    )
    context = context.transpose(1, 0, 2).reshape(rows_here, width)
    attended = matmul_nt(context, attn_out_all) + proj_bias[0]
    normed_one, norm_one_pull = jax.vjp(
        layer_norm, tokens.astype(jnp.float32) + attended, gains[0], shifts[0]
    )
    normed = normed_one.astype(low)
    hidden_pre = matmul(normed, in_all) + hidden_bias
    activated, gelu_pull = jax.vjp(gelu_exact, hidden_pre)
    activated = activated.astype(low)
    mixed = matmul_nt(activated, out_all) + proj_bias[1]
    output, norm_two_pull = jax.vjp(layer_norm, normed_one + mixed, gains[1], shifts[1])
    grad_two, gain_two, shift_two = norm_two_pull(cotangent.astype(jnp.float32))
    grad_mixed = grad_two.astype(low)
    grad_pre = gelu_pull(matmul(grad_mixed, out_all))[0].astype(low)
    grad_normed = matmul_nt(grad_pre, in_all) + grad_two
    grad_one, gain_one, shift_one = norm_one_pull(grad_normed)
    grad_attended = grad_one.astype(low)
    grad_context = matmul(grad_attended, attn_out_all).astype(low)
    grad_context = lax.all_to_all(
        grad_context.reshape(rows_here, members, local).transpose(1, 0, 2),
        "tensor", split_axis=0, concat_axis=0, tiled=False,
    ).reshape(rows_here * members, local)

    def halves(grad):
        grad = lax.psum_scatter(grad.astype(low), "dp", scatter_dimension=0, tiled=True)
        return grad.reshape(part, members, -1).transpose(1, 0, 2)

    grad_out = halves(matmul_tn(grad_mixed, activated))
    grad_in = halves(matmul_tn(normed, grad_pre))
    both = lax.psum_scatter(
        jnp.concatenate([grad_in, grad_out], 1), "tensor", scatter_dimension=0, tiled=False
    ).astype(jnp.float32)
    grad_in, grad_out = both[:part], both[part:]

    grad_queries_t, grad_keys, grad_values = attend_backward(
        ranges, queries_t, queries, keys, keys_t, values, grad_context.T, grad_context,
        context_t, log_sums, seg_q, seg_k, head_dim, block,
    )
    total = dot(grad_queries_t, qkv_all[0], 0, 1)
    total = total + matmul_nt(grad_keys, qkv_all[1])
    total = total + matmul_nt(grad_values, qkv_all[2])
    total = total.astype(low)

    def placed(piece):
        return lax.dynamic_update_slice_in_dim(
            jnp.zeros((width,), jnp.float32), piece, position * local, 0
        )

    sums = jnp.stack(
        [
            placed(jnp.sum(grad_queries_t.astype(jnp.float32), 1)),
            placed(column_sum(grad_values)),
            column_sum(grad_attended),
            column_sum(grad_mixed),
            gain_one,
            gain_two,
            shift_one,
            shift_two,
        ]
    )
    sums = jnp.concatenate(
        [
            sums.reshape(8, groups, part).transpose(1, 0, 2).reshape(groups, 8 * part),
            column_sum(grad_pre).reshape(groups, -1),
        ],
        1,
    ).astype(low)
    amount = sums.shape[1]
    last = jnp.concatenate(
        [
            dot(inputs, grad_queries_t, 0, 1).astype(low),
            matmul_tn(inputs, grad_keys).astype(low),
            matmul_tn(inputs, grad_values).astype(low),
            matmul_tn(grad_attended, context).astype(low),
        ],
        1,
    )
    across = last.shape[1]
    extra = -(-amount // across)
    extra += -extra % 16
    sums = jnp.pad(sums, ((0, 0), (0, extra * across - amount)))
    last = jnp.concatenate(
        [last.reshape(groups, part, across), sums.reshape(groups, extra, across)], 1
    )
    total, last = lax.optimization_barrier((total, last))
    last = lax.psum_scatter(last, "dp", scatter_dimension=0, tiled=False)
    total = lax.all_to_all(
        total.reshape(members, rows_here, width),
        "tensor", split_axis=0, concat_axis=0, tiled=False,
    )
    grad_tokens = (jnp.sum(total.astype(jnp.float32), 0) + grad_one).astype(low)
    grad_qkv = last[:part, : 3 * local].reshape(part, 3, local).transpose(1, 0, 2)
    grad_qkv = grad_qkv.astype(jnp.float32)
    sums = last[part:].reshape(-1)[:amount]
    lines = -(-amount // local)
    sums = jnp.pad(sums, (0, lines * local - amount)).reshape(1, lines, local)
    final = jnp.concatenate(
        [
            last[:part, 3 * local :].reshape(part, members, local).transpose(1, 0, 2),
            jnp.broadcast_to(sums, (members, lines, local)),
        ],
        1,
    )
    final = lax.all_to_all(final, "tensor", split_axis=0, concat_axis=0, tiled=False)
    final = jnp.sum(final.astype(jnp.float32), 0)
    grad_attn_out = final[:part]
    sums = final[part:].reshape(-1)[:amount]
    pieces = sums[: 8 * part].reshape(8, part)
    return (
        output.astype(low),
        grad_tokens,
        grad_qkv,
        grad_attn_out,
        grad_in,
        grad_out,
        pieces[0:2],
        pieces[2:4],
        sums[8 * part :],
        pieces[4:6],
        pieces[6:8],
    )


def solution(mesh):
    in_specs = (
        P(("dp", "tensor"), None),
        P(None, "dp", "tensor"),
        P("dp", "tensor"),
        P("dp", "tensor"),
        P("dp", "tensor"),
        P(None, "dp"),
        P(None, "dp"),
        P("dp"),
        P(None, "dp"),
        P(None, "dp"),
        P("dp", None),
        P(("dp", "tensor"), None),
    )
    out_specs = (
        P(("dp", "tensor"), None),
        P(("dp", "tensor"), None),
        P(None, "dp", "tensor"),
        P("dp", "tensor"),
        P("dp", "tensor"),
        P("dp", "tensor"),
        P(None, "dp"),
        P(None, "dp"),
        P("dp"),
        P(None, "dp"),
        P(None, "dp"),
    )
    return jax.shard_map(
        on_device, mesh=mesh, in_specs=in_specs, out_specs=out_specs, check_vma=False
    )
```
